32 devices in a mesh: replica: 8 (over y, x, core), group: 4 (over z).
Axes of the slice: x: 2, y: 2, z: 4, core: 2. Of those that a mesh axis runs over, the one named last changes fastest.
Arguments:
- layer_input: bfloat16 [8192, 1024], P(('replica', 'group')), may hold values from -6 to 6
- qkv_weight: bfloat16 [1024, 3072], P('group'), may hold values from -0.1875 to 0.1875
- query_bias: bfloat16 [1024], P('group'), may hold values from -3 to 3
- value_bias: bfloat16 [1024], P('group'), may hold values from -3 to 3
- attn_weight: bfloat16 [1024, 1024], P('group'), may hold values from -0.5 to 0.5
- attn_bias: bfloat16 [1024], P('group'), may hold values from -1.75 to 1.75
- first_gain: bfloat16 [1024], P('group'), may hold values from 0.5 to 1.5
- first_shift: bfloat16 [1024], P('group'), may hold values from -1.75 to 1.75
- inner_weight: bfloat16 [1024, 4096], P('group'), may hold values from -0.1875 to 0.1875
- inner_bias: bfloat16 [4096], P('group'), may hold values from -3 to 3
- outer_weight: bfloat16 [4096, 1024], P('group'), may hold values from -0.09375 to 0.09375
- outer_bias: bfloat16 [1024], P('group'), may hold values from -1.75 to 1.75
- second_gain: bfloat16 [1024], P('group'), may hold values from 0.5 to 1.5
- second_shift: bfloat16 [1024], P('group'), may hold values from -1.75 to 1.75
- segment_ids: int32 [8192], P('replica'), may hold values from 0 to 6, as said below
- output_grad: bfloat16 [8192, 1024], P(('replica', 'group')), may hold values from -6 to 6
Outputs:
- layer_output: bfloat16 [8192, 1024], P(('replica', 'group'))
- input_grad: bfloat16 [8192, 1024], P(('replica', 'group'))
- qkv_weight_grad: float32 [1024, 3072], P('group')
- query_bias_grad: float32 [1024], P('group')
- value_bias_grad: float32 [1024], P('group')
- attn_weight_grad: float32 [1024, 1024], P('group')
- attn_bias_grad: float32 [1024], P('group')
- first_gain_grad: float32 [1024], P('group')
- first_shift_grad: float32 [1024], P('group')
- inner_weight_grad: float32 [1024, 4096], P('group')
- inner_bias_grad: float32 [4096], P('group')
- outer_weight_grad: float32 [4096, 1024], P('group')
- outer_bias_grad: float32 [1024], P('group')
- second_gain_grad: float32 [1024], P('group')
- second_shift_grad: float32 [1024], P('group')
The draws below stay inside these ranges and needn't reach their ends.
Inputs may be any that keep to these rules, and one draw needn't show every extreme that they name: `segment_ids`: within each aligned run of 1024 tokens the ids never fall; tokens of different runs never attend to each other.
All inputs are finite; a program needn't handle non-finite values.
Results may differ from the reference program's by a relative error of at most 0.02.
Values may be sent and summed in bfloat16 or wider, within the bound.
A program may use at most 192 MiB of HBM per device.

```python
import jax
import jax.numpy as jnp
from jax import lax

D = 1024
HEADS = 16
HD = 64
FF = 4096
ROWS = 256
LEN = 1024
TOKENS = 8192


def draw_segment_ids(key, part):
    key = jax.random.fold_in(key, 7)
    first_key, last_key = jax.random.split(key)
    run_count = TOKENS // LEN
    half_rows = max(ROWS // 2, 1)
    first_cuts = jax.random.randint(first_key, (run_count, 3), 1, half_rows + 1)
    last_cuts = jax.random.randint(last_key, (run_count, 3), LEN - half_rows, LEN)
    cut_points = jnp.concatenate([first_cuts, last_cuts], axis=1)
    positions = jnp.arange(LEN, dtype=jnp.int32)
    starts = jnp.any(positions[None, None, :] == cut_points[:, :, None], axis=1).astype(jnp.int32)
    return jnp.cumsum(starts, axis=1).reshape(TOKENS).astype(jnp.int32)


def block_levels(own_key, extent, cuts, least, top_value):
    level = 1.0
    for axis_at, shards_of in cuts:
        steps = jax.random.uniform(jax.random.fold_in(jax.random.fold_in(own_key, 6), axis_at), (shards_of,), jnp.float32, least / len(cuts), top_value / len(cuts))
        level = level * jnp.repeat(jnp.exp(steps), extent[axis_at] // shards_of).reshape((-1,) + (1,) * (len(extent) - 1 - axis_at))
    return level


def gaussian(stream_key, extent, width, most, cuts=(), kind=jnp.bfloat16):
    level = block_levels(stream_key, extent, cuts, -0.22, 0.18) if cuts else 1.0
    values = jax.random.normal(stream_key, extent, jnp.float32) * width * level
    return jnp.minimum(jnp.maximum(values, -most), most).astype(kind)


def setup_inputs(seed: int = 0) -> dict:
    seeds = jax.random.split(jax.random.key(seed), 17)
    return {
        "layer_input": gaussian(seeds[0], (TOKENS, D), 1.0, 6.0, ((0, 32),)),
        "qkv_weight": gaussian(seeds[1], (D, 3 * D), D ** -0.5, 0.1875, ((0, 4),)),
        "query_bias": gaussian(seeds[2], (D,), 0.5, 3.0, ((0, 4),)),
        "value_bias": gaussian(seeds[3], (D,), 0.5, 3.0, ((0, 4),)),
        "attn_weight": gaussian(seeds[4], (D, D), (D // 8) ** -0.5, 0.5, ((0, 4),)),
        "attn_bias": gaussian(seeds[5], (D,), 0.3, 1.75, ((0, 4),)),
        "first_gain": jnp.clip(1.0 + 0.1 * jax.random.normal(seeds[6], (D,), jnp.float32), 0.5, 1.5).astype(jnp.bfloat16),
        "first_shift": gaussian(seeds[7], (D,), 0.3, 1.75, ((0, 4),)),
        "inner_weight": gaussian(seeds[8], (D, FF), D ** -0.5, 0.1875, ((0, 4),)),
        "inner_bias": gaussian(seeds[9], (FF,), 0.5, 3.0, ((0, 4),)),
        "outer_weight": gaussian(seeds[10], (FF, D), FF ** -0.5, 0.09375, ((0, 4),)),
        "outer_bias": gaussian(seeds[11], (D,), 0.3, 1.75, ((0, 4),)),
        "second_gain": jnp.clip(1.0 + 0.1 * jax.random.normal(seeds[12], (D,), jnp.float32), 0.5, 1.5).astype(jnp.bfloat16),
        "second_shift": gaussian(seeds[13], (D,), 0.3, 1.75, ((0, 4),)),
        "segment_ids": draw_segment_ids(jax.random.fold_in(seeds[16], 71), 0),
        "output_grad": gaussian(seeds[15], (TOKENS, D), 1.0, 6.0, ((0, 32),)),
    }


NORM_EPS = 1e-05

@jax.custom_vjp
def low(v):
    return lax.optimization_barrier(v.astype(jnp.bfloat16)).astype(jnp.float32)

@jax.custom_vjp
def low_back(v):
    return v

def low_keep(v):
    return (low(v), None)

def low_pass(kept, grad):
    return (grad,)

def back_keep(v):
    return (v, None)

def back_low(kept, grad):
    return (low(grad),)
low.defvjp(low_keep, low_pass)
low_back.defvjp(back_keep, back_low)

def layer_norm(resid, gain, shift):
    average = lax.optimization_barrier(jnp.mean(resid, axis=-1, keepdims=True))
    centred = resid - average
    variance = lax.optimization_barrier(jnp.mean(centred * centred, axis=-1, keepdims=True))
    return centred * lax.rsqrt(variance + NORM_EPS) * gain + shift

def matmul(left, right):
    return jnp.dot(left, right, precision=lax.Precision.HIGHEST, preferred_element_type=jnp.float32)

def attend_head(queries, key_rows, value_rows, allowed):
    scores = low_back(matmul(queries, key_rows.T))
    scores = jnp.where(allowed, scores, -1e+30)
    probs = low(jax.nn.softmax(scores, axis=-1))
    return matmul(probs, value_rows)

def split_heads(matrix):
    return matrix.reshape(matrix.shape[0], HEADS, HD).transpose(1, 0, 2)

def forward(parameters, hidden_in, allowed):
    qkv_w, query_b, value_b, attn_w, attn_b, gain_one, shift_one, inner_w, inner_b, outer_w, outer_b, gain_two, shift_two = parameters
    projected = matmul(hidden_in, qkv_w)
    queries = low_back(low((projected[:, :D] + query_b) * HD ** (-0.5)))
    key_rows = low_back(low(projected[:, D:2 * D]))
    value_rows = low_back(low(projected[:, 2 * D:] + value_b))
    checked = jax.checkpoint(attend_head)

    def one_head(triple):
        return checked(triple[0], triple[1], triple[2], allowed)
    heads_out = lax.map(one_head, (split_heads(queries), split_heads(key_rows), split_heads(value_rows)))
    attended = low_back(low(heads_out.transpose(1, 0, 2).reshape(hidden_in.shape[0], D)))
    branch = low_back(matmul(attended, attn_w) + attn_b)
    first = layer_norm(hidden_in + branch, gain_one, shift_one)
    inner = low_back(matmul(low(first), inner_w) + inner_b)
    activated = low(jax.nn.gelu(inner, approximate=False))
    outer = low_back(matmul(activated, outer_w) + outer_b)
    return layer_norm(first + outer, gain_two, shift_two)

def reference(layer_input, qkv_weight, query_bias, value_bias, attn_weight, attn_bias, first_gain, first_shift, inner_weight, inner_bias, outer_weight, outer_bias, second_gain, second_shift, segment_ids, output_grad):
    parameters = tuple((item.astype(jnp.float32) for item in (qkv_weight, query_bias, value_bias, attn_weight, attn_bias, first_gain, first_shift, inner_weight, inner_bias, outer_weight, outer_bias, second_gain, second_shift)))
    run_count = TOKENS // LEN
    input_rows = layer_input.astype(jnp.float32).reshape(run_count, LEN, D)
    id_rows = segment_ids.reshape(run_count, LEN)
    grad_rows = output_grad.astype(jnp.float32).reshape(run_count, LEN, D)

    def one_run(carry, packed):
        hidden_in, run_ids, cotangent = packed
        allowed = run_ids[:, None] == run_ids[None, :]

        def apply_layer(params_in, activations):
            return forward(params_in, activations, allowed)
        result, pullback = jax.vjp(apply_layer, parameters, hidden_in)
        param_grads, input_grads = pullback(cotangent)
        carry = jax.tree.map(jnp.add, carry, param_grads)
        return (carry, (result.astype(jnp.bfloat16), input_grads.astype(jnp.bfloat16)))
    zeros = jax.tree.map(jnp.zeros_like, parameters)
    totals, (outputs, input_grads) = lax.scan(one_run, zeros, (input_rows, id_rows, grad_rows))
    return (outputs.reshape(TOKENS, D), input_grads.reshape(TOKENS, D), totals[0], totals[1], totals[2], totals[3], totals[4], totals[5], totals[6], totals[7], totals[8], totals[9], totals[10], totals[11], totals[12])
```

```python
import jax
import jax.numpy as jnp
from jax import lax
from jax.sharding import PartitionSpec as P

D = 1024
HEADS = 16
HD = 64


NORM_EPS = 1e-05


def layer_norm(resid, gain, shift):
    average = jnp.mean(resid, axis=-1, keepdims=True)
    centred = resid - average
    variance = jnp.mean(centred * centred, axis=-1, keepdims=True)
    return centred * lax.rsqrt(variance + NORM_EPS) * gain + shift


def gelu_exact(values):
    return jax.nn.gelu(values, approximate=False)


def matmul(left, right):
    return jnp.dot(left, right, preferred_element_type=jnp.float32)


def on_device(
    layer_input,
    qkv_weight,
    query_bias,
    value_bias,
    attn_weight,
    attn_bias,
    first_gain,
    first_shift,
    inner_weight,
    inner_bias,
    outer_weight,
    outer_bias,
    second_gain,
    second_shift,
    segment_ids,
    output_grad,
):
    groups, replicas = lax.axis_size("group"), lax.axis_size("replica")
    group_place, replica_place = lax.axis_index("group"), lax.axis_index("replica")
    row_count = layer_input.shape[0]
    length = segment_ids.shape[0]
    own = query_bias.shape[0]
    hidden = inner_bias.shape[0]
    heads = own // HD
    piece = own // replicas
    score_scale = HD ** (-0.5)

    qkv_rows = lax.dynamic_slice_in_dim(qkv_weight, replica_place * piece, piece)
    inner_rows = lax.dynamic_slice_in_dim(inner_weight, replica_place * piece, piece)
    qkv_rows = qkv_rows.reshape(piece, 3, groups, own).transpose(2, 0, 1, 3)
    inner_rows = inner_rows.reshape(piece, groups, hidden).transpose(1, 0, 2)
    moved = jnp.concatenate([qkv_rows.reshape(groups, piece, 3 * own), inner_rows], axis=2)
    moved = lax.all_to_all(moved, "group", split_axis=0, concat_axis=0, tiled=True)

    def spread(shares):
        every = lax.all_gather(shares, "replica", axis=0)
        return every.transpose(1, 0, 2, 3).reshape(D, shares.shape[-1])

    qkv_cols = spread(moved[:, :, : 3 * own])
    input_all = lax.all_gather(layer_input, "group", axis=0, tiled=True)
    inner_cols = spread(moved[:, :, 3 * own :])
    vectors = jnp.stack(
        [attn_bias, first_gain, first_shift, outer_bias, second_gain, second_shift]
    )
    vectors = lax.all_gather(vectors, "group", axis=0).transpose(1, 0, 2).reshape(6, D)
    attn_bias_full, gain_one, shift_one, outer_bias_full, gain_two, shift_two = vectors

    projected = matmul(input_all, qkv_cols)
    queries = ((projected[:, :own] + query_bias) * score_scale).astype(jnp.bfloat16)
    key_rows = projected[:, own : 2 * own].astype(jnp.bfloat16)
    value_rows = (projected[:, 2 * own :] + value_bias).astype(jnp.bfloat16)
    allowed = segment_ids[:, None] == segment_ids[None, :]
    query_heads = queries.reshape(length, heads, HD)
    key_heads = key_rows.reshape(length, heads, HD)
    value_heads = value_rows.reshape(length, heads, HD)

    def masked_scores():
        raw = jnp.einsum("qhd,khd->hqk", query_heads, key_heads, preferred_element_type=jnp.float32)
        return jnp.where(allowed[None], raw, -1e30)

    scores = masked_scores()
    row_peak = jnp.max(scores, axis=-1, keepdims=True)
    exponent = jnp.exp(scores - row_peak)
    row_total = jnp.sum(exponent, axis=-1, keepdims=True)
    log_total = row_peak + jnp.log(row_total)
    attn_probs = (exponent / row_total).astype(jnp.bfloat16)
    attended = jnp.einsum(
        "hqk,khd->qhd", attn_probs, value_heads, preferred_element_type=jnp.float32
    )
    attended = attended.reshape(length, own).astype(jnp.bfloat16)

    def to_owner(terms):
        return lax.psum_scatter(
            terms.astype(jnp.bfloat16), "group", scatter_dimension=0, tiled=True
        ).astype(jnp.float32)

    def to_all(rows):
        return lax.all_gather(rows, "group", axis=0, tiled=True)

    branch = to_owner(matmul(attended, attn_weight)) + attn_bias_full
    residual_one = layer_input.astype(jnp.float32) + branch
    first, first_pull = jax.vjp(
        layer_norm, residual_one, gain_one.astype(jnp.float32), shift_one.astype(jnp.float32)
    )
    first_all = to_all(first.astype(jnp.bfloat16))
    inner = matmul(first_all, inner_cols) + inner_bias
    activated_f, gelu_pull = jax.vjp(gelu_exact, inner)
    activated = activated_f.astype(jnp.bfloat16)
    outer = to_owner(matmul(activated, outer_weight)) + outer_bias_full
    result, second_pull = jax.vjp(
        layer_norm, first + outer, gain_two.astype(jnp.float32), shift_two.astype(jnp.float32)
    )
    layer_output = result.astype(jnp.bfloat16)
    second_res_grad, second_gain_grad, second_shift_grad = second_pull(
        output_grad.astype(jnp.float32)
    )
    outer_grad = second_res_grad.astype(jnp.bfloat16)
    outer_bias_grad = jnp.sum(outer_grad.astype(jnp.float32), axis=0)
    outer_all = to_all(outer_grad)
    inner_grad = gelu_pull(matmul(outer_all, outer_weight.T))[0].astype(jnp.bfloat16)
    inner_bias_grad = jnp.sum(inner_grad.astype(jnp.float32), axis=0)
    first_grad = second_res_grad + to_owner(matmul(inner_grad, inner_cols.T))
    outer_weight_grad = matmul(activated.T, outer_all).astype(jnp.bfloat16)
    outer_weight_grad = lax.psum(outer_weight_grad, "replica").astype(jnp.float32)

    def to_rows(columns):
        width = columns.shape[-1]
        parts = columns.astype(jnp.bfloat16).reshape(groups, replicas, piece, width)
        parts = parts.transpose(1, 0, 2, 3)
        summed = lax.psum_scatter(parts, "replica", scatter_dimension=0)
        summed = lax.all_to_all(summed, "group", split_axis=0, concat_axis=0, tiled=True)
        return lax.all_gather(summed, "replica", axis=0)

    inner_weight_grad = to_rows(matmul(first_all.T, inner_grad))
    inner_weight_grad = inner_weight_grad.transpose(0, 2, 1, 3).reshape(own, groups * hidden)
    inner_weight_grad = inner_weight_grad.astype(jnp.float32)

    first_res_grad, first_gain_grad, first_shift_grad = first_pull(first_grad)
    branch_grad = first_res_grad.astype(jnp.bfloat16)
    attn_bias_grad = jnp.sum(branch_grad.astype(jnp.float32), axis=0)
    branch_all = to_all(branch_grad)
    attended_grad = matmul(branch_all, attn_weight.T).astype(jnp.bfloat16)
    attended_grad = attended_grad.reshape(length, heads, HD)
    attn_weight_grad = matmul(attended.T, branch_all).astype(jnp.bfloat16)
    attn_weight_grad = lax.psum(attn_weight_grad, "replica").astype(jnp.float32)

    probs = jnp.exp(masked_scores() - log_total)
    probs_low = probs.astype(jnp.bfloat16)
    probs_grad = jnp.einsum(
        "qhd,khd->hqk", attended_grad, value_heads, preferred_element_type=jnp.float32
    )
    values_grad = jnp.einsum(
        "hqk,qhd->khd", probs_low, attended_grad, preferred_element_type=jnp.float32
    )
    weighted = jnp.sum(probs * probs_grad, axis=-1, keepdims=True)
    scores_grad = (probs * (probs_grad - weighted)).astype(jnp.bfloat16)
    queries_grad = jnp.einsum(
        "hqk,khd->qhd", scores_grad, key_heads, preferred_element_type=jnp.float32
    )
    keys_grad = jnp.einsum(
        "hqk,qhd->khd", scores_grad, query_heads, preferred_element_type=jnp.float32
    )
    queries_grad = queries_grad.reshape(length, own).astype(jnp.bfloat16)
    scaled_queries = (queries_grad.astype(jnp.float32) * score_scale).astype(jnp.bfloat16)
    keys_grad = keys_grad.reshape(length, own).astype(jnp.bfloat16)
    values_grad = values_grad.reshape(length, own).astype(jnp.bfloat16)
    projected_grad = jnp.concatenate([scaled_queries, keys_grad, values_grad], axis=1)
    input_terms = to_owner(matmul(projected_grad, qkv_cols.T))
    input_grad = (first_res_grad + input_terms).astype(jnp.bfloat16)
    qkv_weight_grad = to_rows(matmul(input_all.T, projected_grad))
    qkv_weight_grad = qkv_weight_grad.reshape(replicas, groups, piece, 3, own)
    qkv_weight_grad = qkv_weight_grad.transpose(0, 2, 3, 1, 4).reshape(own, 3 * D)
    qkv_weight_grad = qkv_weight_grad.astype(jnp.float32)

    query_bias_grad = jnp.sum(scaled_queries.astype(jnp.float32), axis=0)
    value_bias_grad = jnp.sum(values_grad.astype(jnp.float32), axis=0)
    shared = jnp.stack(
        [
            attn_bias_grad,
            first_gain_grad,
            first_shift_grad,
            outer_bias_grad,
            second_gain_grad,
            second_shift_grad,
        ]
    )
    shared = shared.reshape(6, groups, own).transpose(1, 0, 2).reshape(groups, 6 * own)
    mine = jnp.concatenate([query_bias_grad, value_bias_grad, inner_bias_grad])
    is_mine = jnp.arange(groups)[:, None] == group_place
    terms = jnp.concatenate([shared, jnp.where(is_mine, mine[None], 0.0)], axis=1)
    terms = lax.psum(terms, ("replica", "group"))
    terms = lax.dynamic_index_in_dim(terms, group_place, keepdims=False)
    small = terms[: 8 * own].reshape(8, own)
    return (
        layer_output,
        input_grad,
        qkv_weight_grad,
        small[6],
        small[7],
        attn_weight_grad,
        small[0],
        small[1],
        small[2],
        inner_weight_grad,
        terms[8 * own :],
        outer_weight_grad,
        small[3],
        small[4],
        small[5],
    )


def solution(mesh):
    in_specs = (
        P(("replica", "group"), None),
        P("group", None),
        P("group"),
        P("group"),
        P("group", None),
        P("group"),
        P("group"),
        P("group"),
        P("group", None),
        P("group"),
        P("group", None),
        P("group"),
        P("group"),
        P("group"),
        P("replica"),
        P(("replica", "group"), None),
    )
    out_specs = (
        P(("replica", "group"), None),
        P(("replica", "group"), None),
        P("group", None),
        P("group"),
        P("group"),
        P("group", None),
        P("group"),
        P("group"),
        P("group"),
        P("group", None),
        P("group"),
        P("group", None),
        P("group"),
        P("group"),
        P("group"),
    )
    return jax.shard_map(
        on_device, mesh=mesh, in_specs=in_specs, out_specs=out_specs, check_vma=False
    )
```

```python
import functools

import jax
import jax.numpy as jnp
from jax import lax
from jax.experimental import pallas as pl
from jax.experimental.pallas import tpu as pltpu
from jax.sharding import PartitionSpec as P

D = 1024
HEADS = 16
HD = 64


NORM_EPS = 1e-05


def layer_norm(resid, gain, shift):
    average = jnp.mean(resid, axis=-1, keepdims=True)
    centred = resid - average
    variance = jnp.mean(centred * centred, axis=-1, keepdims=True)
    return centred * lax.rsqrt(variance + NORM_EPS) * gain + shift


def gelu_exact(values):
    return jax.nn.gelu(values, approximate=False)


def matmul(left, right):
    return jnp.dot(left, right, preferred_element_type=jnp.float32)


MESH = pl.DeviceIdType.MESH
EXTRA = 16


def greet_neighbours(me, n):
    barrier = pltpu.get_barrier_semaphore()

    @pl.when(me > 0)
    def _():
        pl.semaphore_signal(
            barrier, inc=1, device_id={"group": me - 1}, device_id_type=MESH
        )

    @pl.when(me < n - 1)
    def _():
        pl.semaphore_signal(
            barrier, inc=1, device_id={"group": me + 1}, device_id_type=MESH
        )

    peers = jnp.where(me > 0, 1, 0) + jnp.where(me < n - 1, 1, 0)
    pl.semaphore_wait(barrier, peers)


def remote(src, dst, send, recv, target):
    return pltpu.make_async_remote_copy(
        src_ref=src,
        dst_ref=dst,
        send_sem=send,
        recv_sem=recv,
        device_id={"group": target},
        device_id_type=MESH,
    )


def chunk_rows(rows, most):
    step = rows // most if rows % (16 * most) == 0 else rows
    return [(start, step) for start in range(0, rows, step)]


def gather_kernel(n, cuts, x_ref, y_ref, xs_ref, ys_ref, send_sem, recv_sem):
    me = lax.axis_index("group")
    rows, extra = x_ref.shape[0], y_ref.shape[0]
    pieces = [(xs_ref, rows, start, size) for start, size in cuts]
    pieces.append((ys_ref, extra, 0, extra))
    xs_ref[pl.ds(pl.multiple_of(me * rows, rows), rows)] = x_ref[...]
    ys_ref[pl.ds(pl.multiple_of(me * extra, extra), extra)] = y_ref[...]
    greet_neighbours(me, n)

    def copy(way, block, at):
        ref, height, start, size = pieces[at]
        part = ref.at[pl.ds(pl.multiple_of(block * height + start, 16), size)]
        target = me + 1 if way == 0 else me - 1
        return remote(part, part, send_sem.at[way, block, at], recv_sem.at[block, at], target)

    for step in range(n):
        for at in range(len(pieces)):
            for way in range(2):
                block = me - step if way == 0 else me + step
                there = block >= 0 if way == 0 else block < n
                onward = me < n - 1 if way == 0 else me > 0
                if step > 0:

                    @pl.when(there)
                    def _():
                        copy(1 - way, block, at).wait_recv()

                if step < n - 1:

                    @pl.when(jnp.logical_and(there, onward))
                    def _():
                        copy(way, block, at).start()

    for step in range(n - 1):
        for at in range(len(pieces)):
            for way in range(2):
                block = me - step if way == 0 else me + step
                there = block >= 0 if way == 0 else block < n
                onward = me < n - 1 if way == 0 else me > 0

                @pl.when(jnp.logical_and(there, onward))
                def _():
                    copy(way, block, at).wait_send()


def gather_rows(rows, extra, place):
    n = lax.axis_size("group")
    cuts = chunk_rows(rows.shape[0], 4)
    vmem = pl.BlockSpec(memory_space=pltpu.VMEM)
    return pl.pallas_call(
        functools.partial(gather_kernel, n, cuts),
        out_shape=[
            jax.ShapeDtypeStruct((n * rows.shape[0], rows.shape[1]), rows.dtype),
            jax.ShapeDtypeStruct((n * extra.shape[0], extra.shape[1]), extra.dtype),
        ],
        in_specs=[vmem, vmem],
        out_specs=[vmem, vmem],
        scratch_shapes=[
            pltpu.SemaphoreType.DMA((2, n, len(cuts) + 1)),
            pltpu.SemaphoreType.DMA((n, len(cuts) + 1)),
        ],
        compiler_params=pltpu.CompilerParams(
            collective_id=place, has_side_effects=True, vmem_limit_bytes=40 * 2**20
        ),
    )(rows, extra)


def reduce_kernel(n, cuts, x_ref, out_ref, right_ref, left_ref, send_sem, recv_sem):
    me = lax.axis_index("group")
    rows = out_ref.shape[0]
    greet_neighbours(me, n)

    def copy(way, block, at):
        start, size = cuts[at]
        ref = right_ref if way == 0 else left_ref
        part = ref.at[block, pl.ds(start, size)]
        target = me + 1 if way == 0 else me - 1
        return remote(part, part, send_sem.at[way, block, at], recv_sem.at[way, block, at], target)

    for step in range(n - 1):
        for at, (start, size) in enumerate(cuts):
            for way in range(2):
                block = n - 1 - step if way == 0 else step
                ref = right_ref if way == 0 else left_ref
                first = me == 0 if way == 0 else me == n - 1
                passes = me < block if way == 0 else me > block
                mine = x_ref[block * rows + start : block * rows + start + size]

                @pl.when(jnp.logical_and(passes, first))
                def _():
                    ref[block, start : start + size] = mine

                @pl.when(jnp.logical_and(passes, jnp.logical_not(first)))
                def _():
                    copy(way, block, at).wait_recv()
                    held = ref[block, start : start + size].astype(jnp.float32)
                    ref[block, start : start + size] = (
                        held + mine.astype(jnp.float32)
                    ).astype(ref.dtype)

                @pl.when(passes)
                def _():
                    copy(way, block, at).start()

    for at, (start, size) in enumerate(cuts):
        own = pl.ds(pl.multiple_of(me * rows + start, 16), size)
        out_ref[start : start + size] = x_ref[own].astype(jnp.float32)

        @pl.when(me > 0)
        def _():
            copy(0, me, at).wait_recv()
            out_ref[start : start + size] += right_ref[me, start : start + size].astype(
                jnp.float32
            )

        @pl.when(me < n - 1)
        def _():
            copy(1, me, at).wait_recv()
            out_ref[start : start + size] += left_ref[me, start : start + size].astype(
                jnp.float32
            )

    for step in range(n - 1):
        for at in range(len(cuts)):
            for way in range(2):
                block = n - 1 - step if way == 0 else step

                @pl.when(me < block if way == 0 else me > block)
                def _():
                    copy(way, block, at).wait_send()


def reduce_rows(terms, place):
    n = lax.axis_size("group")
    rows, width = terms.shape[0] // n, terms.shape[1]
    cuts = chunk_rows(rows, 4)
    vmem = pl.BlockSpec(memory_space=pltpu.VMEM)
    return pl.pallas_call(
        functools.partial(reduce_kernel, n, cuts),
        out_shape=jax.ShapeDtypeStruct((rows, width), jnp.float32),
        in_specs=[vmem],
        out_specs=vmem,
        scratch_shapes=[
            pltpu.VMEM((n, rows, width), jnp.bfloat16),
            pltpu.VMEM((n, rows, width), jnp.bfloat16),
            pltpu.SemaphoreType.DMA((2, n, len(cuts))),
            pltpu.SemaphoreType.DMA((2, n, len(cuts))),
        ],
        compiler_params=pltpu.CompilerParams(
            collective_id=place, has_side_effects=True, vmem_limit_bytes=40 * 2**20
        ),
    )(terms.astype(jnp.bfloat16))


def exchange_kernel(n, x_ref, out_ref, send_sem, recv_sem):
    me = lax.axis_index("group")
    barrier = pltpu.get_barrier_semaphore()
    for hop in range(1, n):
        pl.semaphore_signal(
            barrier,
            inc=1,
            device_id={"group": lax.rem(me + hop, n)},
            device_id_type=MESH,
        )
    pl.semaphore_wait(barrier, n - 1)
    out_ref[me] = x_ref[me]
    copies = []
    for hop in range(1, n):
        target = lax.rem(me + hop, n)
        copy = remote(
            x_ref.at[target], out_ref.at[me], send_sem.at[hop], recv_sem.at[hop], target
        )
        copy.start()
        copies.append(copy)
    for hop in range(1, n):
        source = lax.rem(me + n - hop, n)
        remote(
            x_ref.at[source],
            out_ref.at[source],
            send_sem.at[hop],
            recv_sem.at[hop],
            source,
        ).wait_recv()
    for copy in copies:
        copy.wait_send()


def exchange(parts, place):
    n = lax.axis_size("group")
    vmem = pl.BlockSpec(memory_space=pltpu.VMEM)
    return pl.pallas_call(
        functools.partial(exchange_kernel, n),
        out_shape=jax.ShapeDtypeStruct(parts.shape, parts.dtype),
        in_specs=[vmem],
        out_specs=vmem,
        scratch_shapes=[pltpu.SemaphoreType.DMA((n,)), pltpu.SemaphoreType.DMA((n,))],
        compiler_params=pltpu.CompilerParams(
            collective_id=place, has_side_effects=True, vmem_limit_bytes=40 * 2**20
        ),
    )(parts)


def on_device(
    layer_input,
    qkv_weight,
    query_bias,
    value_bias,
    attn_weight,
    attn_bias,
    first_gain,
    first_shift,
    inner_weight,
    inner_bias,
    outer_weight,
    outer_bias,
    second_gain,
    second_shift,
    segment_ids,
    output_grad,
):
    groups, replicas = lax.axis_size("group"), lax.axis_size("replica")
    group_place, replica_place = lax.axis_index("group"), lax.axis_index("replica")
    row_count = layer_input.shape[0]
    length = segment_ids.shape[0]
    own = query_bias.shape[0]
    hidden = inner_bias.shape[0]
    heads = own // HD
    piece = own // replicas
    score_scale = HD ** (-0.5)

    qkv_rows = lax.dynamic_slice_in_dim(qkv_weight, replica_place * piece, piece)
    inner_rows = lax.dynamic_slice_in_dim(inner_weight, replica_place * piece, piece)
    qkv_rows = qkv_rows.reshape(piece, 3, groups, own).transpose(2, 0, 1, 3)
    inner_rows = inner_rows.reshape(piece, groups, hidden).transpose(1, 0, 2)
    moved = jnp.concatenate([qkv_rows.reshape(groups, piece, 3 * own), inner_rows], axis=2)
    moved = exchange(moved, 0)

    def spread(shares):
        every = lax.all_gather(shares, "replica", axis=0)
        return every.transpose(1, 0, 2, 3).reshape(D, shares.shape[-1])

    qkv_cols = spread(moved[:, :, : 3 * own])
    inner_cols = spread(moved[:, :, 3 * own :])
    vectors = jnp.stack(
        [attn_bias, first_gain, first_shift, outer_bias, second_gain, second_shift]
    )
    vectors = jnp.pad(vectors, ((0, EXTRA - 6), (0, 0)))
    input_all, vectors = gather_rows(layer_input, vectors, 1)
    vectors = vectors.reshape(groups, EXTRA, own)[:, :6].transpose(1, 0, 2).reshape(6, D)
    attn_bias_full, gain_one, shift_one, outer_bias_full, gain_two, shift_two = vectors

    projected = matmul(input_all, qkv_cols)
    queries = ((projected[:, :own] + query_bias) * score_scale).astype(jnp.bfloat16)
    key_rows = projected[:, own : 2 * own].astype(jnp.bfloat16)
    value_rows = (projected[:, 2 * own :] + value_bias).astype(jnp.bfloat16)
    allowed = segment_ids[:, None] == segment_ids[None, :]
    query_heads = queries.reshape(length, heads, HD)
    key_heads = key_rows.reshape(length, heads, HD)
    value_heads = value_rows.reshape(length, heads, HD)

    def masked_scores():
        raw = jnp.einsum("qhd,khd->hqk", query_heads, key_heads, preferred_element_type=jnp.float32)
        return jnp.where(allowed[None], raw, -1e30)

    scores = masked_scores()
    row_peak = jnp.max(scores, axis=-1, keepdims=True)
    exponent = jnp.exp(scores - row_peak)
    row_total = jnp.sum(exponent, axis=-1, keepdims=True)
    log_total = row_peak + jnp.log(row_total)
    attn_probs = (exponent / row_total).astype(jnp.bfloat16)
    attended = jnp.einsum(
        "hqk,khd->qhd", attn_probs, value_heads, preferred_element_type=jnp.float32
    )
    attended = attended.reshape(length, own).astype(jnp.bfloat16)

    def own_sums(extra):
        sums = jnp.sum(extra.reshape(groups, EXTRA, D)[:, :2].astype(jnp.float32), axis=0)
        return lax.dynamic_slice_in_dim(sums, group_place * own, own, axis=1)

    def own_columns(rows):
        columns = lax.dynamic_slice_in_dim(rows, group_place * own, own, axis=1)
        return jnp.sum(columns.astype(jnp.float32), axis=0)

    def extra_rows(values, width):
        values = jnp.concatenate(values).astype(jnp.bfloat16)
        values = jnp.pad(values, (0, EXTRA * width - values.shape[0]))
        return values.reshape(EXTRA, width)

    branch = reduce_rows(matmul(attended, attn_weight), 2) + attn_bias_full
    residual_one = layer_input.astype(jnp.float32) + branch
    first, first_pull = jax.vjp(
        layer_norm, residual_one, gain_one.astype(jnp.float32), shift_one.astype(jnp.float32)
    )
    empty = jnp.zeros((EXTRA, 128), jnp.bfloat16)
    first_all, _ = gather_rows(first.astype(jnp.bfloat16), empty, 3)
    inner = matmul(first_all, inner_cols) + inner_bias
    activated_f, gelu_pull = jax.vjp(gelu_exact, inner)
    activated = activated_f.astype(jnp.bfloat16)
    outer = reduce_rows(matmul(activated, outer_weight), 4) + outer_bias_full
    result, second_pull = jax.vjp(
        layer_norm, first + outer, gain_two.astype(jnp.float32), shift_two.astype(jnp.float32)
    )
    layer_output = result.astype(jnp.bfloat16)
    second_res_grad, second_gain_grad, second_shift_grad = second_pull(
        output_grad.astype(jnp.float32)
    )
    outer_grad = second_res_grad.astype(jnp.bfloat16)
    outer_all, second_extra = gather_rows(
        outer_grad, extra_rows([second_gain_grad, second_shift_grad], D), 5
    )
    inner_grad = gelu_pull(matmul(outer_all, outer_weight.T))[0].astype(jnp.bfloat16)
    inner_bias_grad = jnp.sum(inner_grad.astype(jnp.float32), axis=0)
    outer_weight_grad = matmul(activated.T, outer_all).astype(jnp.bfloat16)
    early = extra_rows(
        [own_sums(second_extra).reshape(-1), own_columns(outer_all), inner_bias_grad], D
    )
    inner_weight_grad = matmul(first_all.T, inner_grad).astype(jnp.bfloat16)
    outer_weight_grad, inner_weight_grad = lax.psum(
        (jnp.concatenate([outer_weight_grad, early], axis=0), inner_weight_grad), "replica"
    )

    def to_rows(columns, place):
        parts = columns.reshape(groups, replicas, piece, columns.shape[-1])
        parts = lax.dynamic_index_in_dim(parts, replica_place, axis=1, keepdims=False)
        return lax.all_gather(exchange(parts, place), "replica", axis=0)

    inner_rows_grad = to_rows(inner_weight_grad, 6)
    inner_rows_grad = inner_rows_grad.transpose(0, 2, 1, 3).reshape(own, groups * hidden)
    inner_rows_grad = inner_rows_grad.astype(jnp.float32)
    first_grad = second_res_grad + reduce_rows(matmul(inner_grad, inner_cols.T), 7)

    first_res_grad, first_gain_grad, first_shift_grad = first_pull(first_grad)
    branch_grad = first_res_grad.astype(jnp.bfloat16)
    branch_all, first_extra = gather_rows(
        branch_grad, extra_rows([first_gain_grad, first_shift_grad], D), 8
    )
    attended_grad = matmul(branch_all, attn_weight.T).astype(jnp.bfloat16)
    attended_grad = attended_grad.reshape(length, heads, HD)
    attn_weight_grad = matmul(attended.T, branch_all).astype(jnp.bfloat16)

    probs = jnp.exp(masked_scores() - log_total)
    probs_low = probs.astype(jnp.bfloat16)
    probs_grad = jnp.einsum(
        "qhd,khd->hqk", attended_grad, value_heads, preferred_element_type=jnp.float32
    )
    values_grad = jnp.einsum(
        "hqk,qhd->khd", probs_low, attended_grad, preferred_element_type=jnp.float32
    )
    weighted = jnp.sum(probs * probs_grad, axis=-1, keepdims=True)
    scores_grad = (probs * (probs_grad - weighted)).astype(jnp.bfloat16)
    queries_grad = jnp.einsum(
        "hqk,khd->qhd", scores_grad, key_heads, preferred_element_type=jnp.float32
    )
    keys_grad = jnp.einsum(
        "hqk,qhd->khd", scores_grad, query_heads, preferred_element_type=jnp.float32
    )
    queries_grad = queries_grad.reshape(length, own).astype(jnp.bfloat16)
    scaled_queries = (queries_grad.astype(jnp.float32) * score_scale).astype(jnp.bfloat16)
    keys_grad = keys_grad.reshape(length, own).astype(jnp.bfloat16)
    values_grad = values_grad.reshape(length, own).astype(jnp.bfloat16)
    projected_grad = jnp.concatenate([scaled_queries, keys_grad, values_grad], axis=1)
    query_bias_grad = jnp.sum(scaled_queries.astype(jnp.float32), axis=0)
    value_bias_grad = jnp.sum(values_grad.astype(jnp.float32), axis=0)
    late = extra_rows(
        [
            own_sums(first_extra).reshape(-1),
            own_columns(branch_all),
            query_bias_grad,
            value_bias_grad,
        ],
        D,
    )
    attn_weight_grad = jnp.concatenate([attn_weight_grad, late], axis=0)
    last_grad, _, outer_weight_grad = lax.optimization_barrier(
        (projected_grad, inner_weight_grad, outer_weight_grad)
    )
    qkv_weight_grad = matmul(input_all.T, last_grad).astype(jnp.bfloat16)
    qkv_weight_grad, attn_weight_grad = lax.psum((qkv_weight_grad, attn_weight_grad), "replica")
    input_terms = reduce_rows(matmul(projected_grad, qkv_cols.T), 9)
    input_grad = (first_res_grad + input_terms).astype(jnp.bfloat16)
    early = outer_weight_grad[hidden:].reshape(-1).astype(jnp.float32)
    outer_weight_grad = outer_weight_grad[:hidden].astype(jnp.float32)
    late = attn_weight_grad[own:].reshape(-1).astype(jnp.float32)
    attn_weight_grad = attn_weight_grad[:own].astype(jnp.float32)
    qkv_weight_grad = to_rows(qkv_weight_grad, 10)
    qkv_weight_grad = qkv_weight_grad.reshape(replicas, groups, piece, 3, own)
    qkv_weight_grad = qkv_weight_grad.transpose(0, 2, 3, 1, 4).reshape(own, 3 * D)
    qkv_weight_grad = qkv_weight_grad.astype(jnp.float32)
    second_gain_grad, second_shift_grad, outer_bias_grad = early[: 3 * own].reshape(3, own)
    inner_bias_grad = early[3 * own : 3 * own + hidden]
    late = late[: 5 * own].reshape(5, own)
    return (
        layer_output,
        input_grad,
        qkv_weight_grad,
        late[3],
        late[4],
        attn_weight_grad,
        late[2],
        late[0],
        late[1],
        inner_rows_grad,
        inner_bias_grad,
        outer_weight_grad,
        outer_bias_grad,
        second_gain_grad,
        second_shift_grad,
    )


def solution(mesh):
    in_specs = (
        P(("replica", "group"), None),
        P("group", None),
        P("group"),
        P("group"),
        P("group", None),
        P("group"),
        P("group"),
        P("group"),
        P("group", None),
        P("group"),
        P("group", None),
        P("group"),
        P("group"),
        P("group"),
        P("replica"),
        P(("replica", "group"), None),
    )
    out_specs = (
        P(("replica", "group"), None),
        P(("replica", "group"), None),
        P("group", None),
        P("group"),
        P("group"),
        P("group", None),
        P("group"),
        P("group"),
        P("group"),
        P("group", None),
        P("group"),
        P("group", None),
        P("group"),
        P("group"),
        P("group"),
    )
    return jax.shard_map(
        on_device, mesh=mesh, in_specs=in_specs, out_specs=out_specs, check_vma=False
    )
```

```python
import functools

import jax
import jax.numpy as jnp
from jax import lax
from jax.experimental import pallas as pl
from jax.experimental.pallas import tpu as pltpu
from jax.sharding import PartitionSpec as P

D = 1024
HEADS = 16
HD = 64


NORM_EPS = 1e-05


def layer_norm(resid, gain, shift):
    average = jnp.mean(resid, axis=-1, keepdims=True)
    centred = resid - average
    variance = jnp.mean(centred * centred, axis=-1, keepdims=True)
    return centred * lax.rsqrt(variance + NORM_EPS) * gain + shift


def gelu_exact(values):
    return jax.nn.gelu(values, approximate=False)


def matmul(left, right):
    return jnp.dot(left, right, preferred_element_type=jnp.float32)


MESH = pl.DeviceIdType.MESH
EXTRA = 16


def cost(micros):
    return pl.CostEstimate(
        flops=micros * 10**9, bytes_accessed=micros * 3 * 10**6, transcendentals=0
    )


def greet_neighbours(me, n):
    barrier = pltpu.get_barrier_semaphore()

    @pl.when(me > 0)
    def _():
        pl.semaphore_signal(
            barrier, inc=1, device_id={"group": me - 1}, device_id_type=MESH
        )

    @pl.when(me < n - 1)
    def _():
        pl.semaphore_signal(
            barrier, inc=1, device_id={"group": me + 1}, device_id_type=MESH
        )

    peers = jnp.where(me > 0, 1, 0) + jnp.where(me < n - 1, 1, 0)
    pl.semaphore_wait(barrier, peers)


def remote(src, dst, send, recv, target):
    return pltpu.make_async_remote_copy(
        src_ref=src,
        dst_ref=dst,
        send_sem=send,
        recv_sem=recv,
        device_id={"group": target},
        device_id_type=MESH,
    )


def chunk_rows(rows, most):
    step = rows // most if rows % (16 * most) == 0 else rows
    return [(start, step) for start in range(0, rows, step)]


def gather_kernel(n, cuts, x_ref, y_ref, xs_ref, ys_ref, send_sem, recv_sem):
    me = lax.axis_index("group")
    rows, extra = x_ref.shape[0], y_ref.shape[0]
    pieces = [(xs_ref, rows, start, size) for start, size in cuts]
    pieces.append((ys_ref, extra, 0, extra))
    xs_ref[pl.ds(pl.multiple_of(me * rows, rows), rows)] = x_ref[...]
    ys_ref[pl.ds(pl.multiple_of(me * extra, extra), extra)] = y_ref[...]
    greet_neighbours(me, n)

    def copy(way, block, at):
        ref, height, start, size = pieces[at]
        part = ref.at[pl.ds(pl.multiple_of(block * height + start, 16), size)]
        target = me + 1 if way == 0 else me - 1
        return remote(part, part, send_sem.at[way, block, at], recv_sem.at[block, at], target)

    for step in range(n):
        for at in range(len(pieces)):
            for way in range(2):
                block = me - step if way == 0 else me + step
                there = block >= 0 if way == 0 else block < n
                onward = me < n - 1 if way == 0 else me > 0
                if step > 0:

                    @pl.when(there)
                    def _():
                        copy(1 - way, block, at).wait_recv()

                if step < n - 1:

                    @pl.when(jnp.logical_and(there, onward))
                    def _():
                        copy(way, block, at).start()

    for step in range(n - 1):
        for at in range(len(pieces)):
            for way in range(2):
                block = me - step if way == 0 else me + step
                there = block >= 0 if way == 0 else block < n
                onward = me < n - 1 if way == 0 else me > 0

                @pl.when(jnp.logical_and(there, onward))
                def _():
                    copy(way, block, at).wait_send()


def gather_rows(rows, extra, place, micros=25):
    n = lax.axis_size("group")
    cuts = chunk_rows(rows.shape[0], 4)
    vmem = pl.BlockSpec(memory_space=pltpu.VMEM)
    return pl.pallas_call(
        functools.partial(gather_kernel, n, cuts),
        out_shape=[
            jax.ShapeDtypeStruct((n * rows.shape[0], rows.shape[1]), rows.dtype),
            jax.ShapeDtypeStruct((n * extra.shape[0], extra.shape[1]), extra.dtype),
        ],
        in_specs=[vmem, vmem],
        out_specs=[vmem, vmem],
        scratch_shapes=[
            pltpu.SemaphoreType.DMA((2, n, len(cuts) + 1)),
            pltpu.SemaphoreType.DMA((n, len(cuts) + 1)),
        ],
        compiler_params=pltpu.CompilerParams(
            collective_id=place, has_side_effects=True, vmem_limit_bytes=40 * 2**20
        ),
        cost_estimate=cost(micros),
    )(rows, extra)


def reduce_kernel(n, cuts, lag, x_ref, out_ref, held_ref, send_sem, recv_sem):
    me = lax.axis_index("group")
    rows = out_ref.shape[0]
    near = jnp.where(me < n // 2, 0, 1)
    size = cuts[0][1]
    greet_neighbours(me, n)

    def copy(way, block, at):
        part = held_ref.at[way, block, pl.ds(cuts[at][0], size)]
        target = me + 1 - 2 * way
        return remote(part, part, send_sem.at[way, block, at], recv_sem.at[way, block, at], target)

    def place(way, step):
        block = jnp.where(way == 0, n - 1 - step, step)
        first = me == jnp.where(way == 0, 0, n - 1)
        ahead = jnp.where(way == 0, block - me, me - block)
        return block, first, ahead > 0

    def send(way, step, at):
        block, first, passes = place(way, step)
        start = cuts[at][0]
        here = pl.ds(start, size)
        mine = pl.ds(pl.multiple_of(block * rows + start, 16), size)

        @pl.when(jnp.logical_and(passes, first))
        def _():
            held_ref[way, block, here] = x_ref[mine]

        @pl.when(jnp.logical_and(passes, jnp.logical_not(first)))
        def _():
            copy(way, block, at).wait_recv()
            held_ref[way, block, here] = (
                held_ref[way, block, here].astype(jnp.float32) + x_ref[mine].astype(jnp.float32)
            ).astype(held_ref.dtype)

        @pl.when(passes)
        def _():
            copy(way, block, at).start()

    items = [(step, at) for step in range(n - 1) for at in range(len(cuts))]
    for now in range(len(items) + lag):
        if now < len(items):
            send(near, *items[now])
        if now >= lag:
            send(1 - near, *items[now - lag])

    for at, (start, _) in enumerate(cuts):
        here = pl.ds(start, size)
        own = pl.ds(pl.multiple_of(me * rows + start, 16), size)
        out_ref[here] = x_ref[own].astype(jnp.float32)
        for way in range(2):

            @pl.when(me > 0 if way == 0 else me < n - 1)
            def _():
                copy(way, me, at).wait_recv()
                out_ref[here] += held_ref[way, me, here].astype(jnp.float32)

    for step, at in items:
        for way in range(2):
            block, _, passes = place(way, step)

            @pl.when(passes)
            def _():
                copy(way, block, at).wait_send()


def reduce_rows(terms, place, micros=25):
    n = lax.axis_size("group")
    rows, width = terms.shape[0] // n, terms.shape[1]
    cuts = chunk_rows(rows, 4)
    vmem = pl.BlockSpec(memory_space=pltpu.VMEM)
    return pl.pallas_call(
        functools.partial(reduce_kernel, n, cuts, 3),
        out_shape=jax.ShapeDtypeStruct((rows, width), jnp.float32),
        in_specs=[vmem],
        out_specs=vmem,
        scratch_shapes=[
            pltpu.VMEM((2, n, rows, width), jnp.bfloat16),
            pltpu.SemaphoreType.DMA((2, n, len(cuts))),
            pltpu.SemaphoreType.DMA((2, n, len(cuts))),
        ],
        compiler_params=pltpu.CompilerParams(
            collective_id=place, has_side_effects=True, vmem_limit_bytes=40 * 2**20
        ),
        cost_estimate=cost(micros),
    )(terms.astype(jnp.bfloat16))


def exchange_kernel(n, x_ref, out_ref, send_sem, recv_sem):
    me = lax.axis_index("group")
    barrier = pltpu.get_barrier_semaphore()
    for hop in range(1, n):
        pl.semaphore_signal(
            barrier,
            inc=1,
            device_id={"group": lax.rem(me + hop, n)},
            device_id_type=MESH,
        )
    pl.semaphore_wait(barrier, n - 1)
    out_ref[me] = x_ref[me]
    copies = []
    for hop in range(1, n):
        target = lax.rem(me + hop, n)
        copy = remote(
            x_ref.at[target], out_ref.at[me], send_sem.at[hop], recv_sem.at[hop], target
        )
        copy.start()
        copies.append(copy)
    for hop in range(1, n):
        source = lax.rem(me + n - hop, n)
        remote(
            x_ref.at[source],
            out_ref.at[source],
            send_sem.at[hop],
            recv_sem.at[hop],
            source,
        ).wait_recv()
    for copy in copies:
        copy.wait_send()


def exchange(parts, place):
    n = lax.axis_size("group")
    vmem = pl.BlockSpec(memory_space=pltpu.VMEM)
    return pl.pallas_call(
        functools.partial(exchange_kernel, n),
        out_shape=jax.ShapeDtypeStruct(parts.shape, parts.dtype),
        in_specs=[vmem],
        out_specs=vmem,
        scratch_shapes=[pltpu.SemaphoreType.DMA((n,)), pltpu.SemaphoreType.DMA((n,))],
        compiler_params=pltpu.CompilerParams(
            collective_id=place, has_side_effects=True, vmem_limit_bytes=40 * 2**20
        ),
        cost_estimate=cost(8),
    )(parts)


def on_device(
    layer_input,
    qkv_weight,
    query_bias,
    value_bias,
    attn_weight,
    attn_bias,
    first_gain,
    first_shift,
    inner_weight,
    inner_bias,
    outer_weight,
    outer_bias,
    second_gain,
    second_shift,
    segment_ids,
    output_grad,
):
    groups, replicas = lax.axis_size("group"), lax.axis_size("replica")
    group_place, replica_place = lax.axis_index("group"), lax.axis_index("replica")
    row_count = layer_input.shape[0]
    length = segment_ids.shape[0]
    own = query_bias.shape[0]
    hidden = inner_bias.shape[0]
    heads = own // HD
    piece = own // replicas
    score_scale = HD ** (-0.5)

    qkv_rows = lax.dynamic_slice_in_dim(qkv_weight, replica_place * piece, piece)
    inner_rows = lax.dynamic_slice_in_dim(inner_weight, replica_place * piece, piece)
    qkv_rows = qkv_rows.reshape(piece, 3, groups, own).transpose(2, 0, 1, 3)
    inner_rows = inner_rows.reshape(piece, groups, hidden).transpose(1, 0, 2)
    moved = jnp.concatenate([qkv_rows.reshape(groups, piece, 3 * own), inner_rows], axis=2)
    moved = exchange(moved, 0)

    def spread(shares):
        every = lax.all_gather(shares, "replica", axis=0)
        return every.transpose(1, 0, 2, 3).reshape(D, shares.shape[-1])

    qkv_cols = spread(moved[:, :, : 3 * own])
    inner_cols = spread(moved[:, :, 3 * own :])
    vectors = jnp.stack(
        [attn_bias, first_gain, first_shift, outer_bias, second_gain, second_shift]
    )
    vectors = jnp.pad(vectors, ((0, EXTRA - 6), (0, 0)))
    input_all, vectors = gather_rows(layer_input, vectors, 1)
    vectors = vectors.reshape(groups, EXTRA, own)[:, :6].transpose(1, 0, 2).reshape(6, D)
    attn_bias_full, gain_one, shift_one, outer_bias_full, gain_two, shift_two = vectors

    projected = matmul(input_all, qkv_cols)
    queries = ((projected[:, :own] + query_bias) * score_scale).astype(jnp.bfloat16)
    key_rows = projected[:, own : 2 * own].astype(jnp.bfloat16)
    value_rows = (projected[:, 2 * own :] + value_bias).astype(jnp.bfloat16)
    allowed = segment_ids[:, None] == segment_ids[None, :]
    query_heads = queries.reshape(length, heads, HD)
    key_heads = key_rows.reshape(length, heads, HD)
    value_heads = value_rows.reshape(length, heads, HD)

    def masked_scores():
        raw = jnp.einsum("qhd,khd->hqk", query_heads, key_heads, preferred_element_type=jnp.float32)
        return jnp.where(allowed[None], raw, -1e30)

    scores = masked_scores()
    row_peak = jnp.max(scores, axis=-1, keepdims=True)
    exponent = jnp.exp(scores - row_peak)
    row_total = jnp.sum(exponent, axis=-1, keepdims=True)
    log_total = row_peak + jnp.log(row_total)
    attn_probs = (exponent / row_total).astype(jnp.bfloat16)
    attended = jnp.einsum(
        "hqk,khd->qhd", attn_probs, value_heads, preferred_element_type=jnp.float32
    )
    attended = attended.reshape(length, own).astype(jnp.bfloat16)

    def own_sums(extra):
        sums = jnp.sum(extra.reshape(groups, EXTRA, D)[:, :2].astype(jnp.float32), axis=0)
        return lax.dynamic_slice_in_dim(sums, group_place * own, own, axis=1)

    def own_columns(rows):
        columns = lax.dynamic_slice_in_dim(rows, group_place * own, own, axis=1)
        return jnp.sum(columns.astype(jnp.float32), axis=0)

    def extra_rows(values, width):
        values = jnp.concatenate(values).astype(jnp.bfloat16)
        values = jnp.pad(values, (0, EXTRA * width - values.shape[0]))
        return values.reshape(EXTRA, width)

    branch = reduce_rows(matmul(attended, attn_weight), 2) + attn_bias_full
    residual_one = layer_input.astype(jnp.float32) + branch
    first, first_pull = jax.vjp(
        layer_norm, residual_one, gain_one.astype(jnp.float32), shift_one.astype(jnp.float32)
    )
    empty = jnp.zeros((EXTRA, 128), jnp.bfloat16)
    first_all, _ = gather_rows(first.astype(jnp.bfloat16), empty, 3)
    inner = matmul(first_all, inner_cols) + inner_bias
    activated_f, gelu_pull = jax.vjp(gelu_exact, inner)
    activated = activated_f.astype(jnp.bfloat16)
    outer = reduce_rows(matmul(activated, outer_weight), 4) + outer_bias_full
    result, second_pull = jax.vjp(
        layer_norm, first + outer, gain_two.astype(jnp.float32), shift_two.astype(jnp.float32)
    )
    layer_output = result.astype(jnp.bfloat16)
    second_res_grad, second_gain_grad, second_shift_grad = second_pull(
        output_grad.astype(jnp.float32)
    )
    outer_grad = second_res_grad.astype(jnp.bfloat16)
    outer_all, second_extra = gather_rows(
        outer_grad, extra_rows([second_gain_grad, second_shift_grad], D), 5
    )
    inner_grad = gelu_pull(matmul(outer_all, outer_weight.T))[0].astype(jnp.bfloat16)
    inner_bias_grad = jnp.sum(inner_grad.astype(jnp.float32), axis=0)
    outer_weight_grad = matmul(activated.T, outer_all).astype(jnp.bfloat16)
    early = extra_rows(
        [own_sums(second_extra).reshape(-1), own_columns(outer_all), inner_bias_grad], D
    )
    inner_weight_grad = matmul(first_all.T, inner_grad).astype(jnp.bfloat16)
    outer_weight_grad = jnp.concatenate([outer_weight_grad, early], axis=0)
    outer_weight_grad, inner_weight_grad, later_grad = lax.optimization_barrier(
        (outer_weight_grad, inner_weight_grad, inner_grad)
    )
    outer_weight_grad, inner_weight_grad = lax.psum(
        (outer_weight_grad, inner_weight_grad), "replica"
    )

    def to_rows(columns, sections, place):
        width = columns.shape[-1]
        parts = columns.reshape(groups, replicas, piece, width)
        parts = lax.dynamic_index_in_dim(parts, replica_place, axis=1, keepdims=False)
        parts = exchange(parts, place).reshape(groups, piece, sections, width // sections)
        parts = parts.transpose(1, 2, 0, 3).reshape(piece, groups * width)
        whole_rows = lax.all_gather(parts, "replica", axis=0, tiled=True)
        return whole_rows.astype(jnp.float32)

    first_grad = second_res_grad + reduce_rows(matmul(later_grad, inner_cols.T), 7, 0)

    first_res_grad, first_gain_grad, first_shift_grad = first_pull(first_grad)
    branch_grad = first_res_grad.astype(jnp.bfloat16)
    branch_all, first_extra = gather_rows(
        branch_grad, extra_rows([first_gain_grad, first_shift_grad], D), 8, 0
    )
    attended_grad = matmul(branch_all, attn_weight.T).astype(jnp.bfloat16)
    attended_grad, inner_weight_grad, outer_weight_grad, branch_all = lax.optimization_barrier(
        (attended_grad, inner_weight_grad, outer_weight_grad, branch_all)
    )
    attn_weight_grad = matmul(attended.T, branch_all).astype(jnp.bfloat16)
    attended_grad = attended_grad.reshape(length, heads, HD)

    probs = jnp.exp(masked_scores() - log_total)
    probs_low = probs.astype(jnp.bfloat16)
    probs_grad = jnp.einsum(
        "qhd,khd->hqk", attended_grad, value_heads, preferred_element_type=jnp.float32
    )
    values_grad = jnp.einsum(
        "hqk,qhd->khd", probs_low, attended_grad, preferred_element_type=jnp.float32
    )
    weighted = jnp.sum(probs * probs_grad, axis=-1, keepdims=True)
    scores_grad = (probs * (probs_grad - weighted)).astype(jnp.bfloat16)
    queries_grad = jnp.einsum(
        "hqk,khd->qhd", scores_grad, key_heads, preferred_element_type=jnp.float32
    )
    keys_grad = jnp.einsum(
        "hqk,qhd->khd", scores_grad, query_heads, preferred_element_type=jnp.float32
    )
    queries_grad = queries_grad.reshape(length, own).astype(jnp.bfloat16)
    scaled_queries = (queries_grad.astype(jnp.float32) * score_scale).astype(jnp.bfloat16)
    keys_grad = keys_grad.reshape(length, own).astype(jnp.bfloat16)
    values_grad = values_grad.reshape(length, own).astype(jnp.bfloat16)
    projected_grad = jnp.concatenate([scaled_queries, keys_grad, values_grad], axis=1)
    query_bias_grad = jnp.sum(scaled_queries.astype(jnp.float32), axis=0)
    value_bias_grad = jnp.sum(values_grad.astype(jnp.float32), axis=0)
    late = extra_rows(
        [
            own_sums(first_extra).reshape(-1),
            own_columns(branch_all),
            query_bias_grad,
            value_bias_grad,
        ],
        D,
    )
    attn_weight_grad = jnp.concatenate([attn_weight_grad, late], axis=0)
    inner_rows_grad = to_rows(inner_weight_grad, 1, 6)
    qkv_weight_grad = matmul(input_all.T, projected_grad).astype(jnp.bfloat16)
    qkv_weight_grad, attn_weight_grad = lax.psum((qkv_weight_grad, attn_weight_grad), "replica")
    input_terms = reduce_rows(matmul(projected_grad, qkv_cols.T), 9)
    input_grad = (first_res_grad + input_terms).astype(jnp.bfloat16)
    early = outer_weight_grad[hidden:].reshape(-1).astype(jnp.float32)
    outer_weight_grad = outer_weight_grad[:hidden].astype(jnp.float32)
    qkv_weight_grad, attn_weight_grad, input_grad = lax.optimization_barrier(
        (qkv_weight_grad, attn_weight_grad, input_grad)
    )
    late = attn_weight_grad[own:].reshape(-1).astype(jnp.float32)
    attn_weight_grad = attn_weight_grad[:own].astype(jnp.float32)
    qkv_weight_grad = to_rows(qkv_weight_grad, 3, 10)
    second_gain_grad, second_shift_grad, outer_bias_grad = early[: 3 * own].reshape(3, own)
    inner_bias_grad = early[3 * own : 3 * own + hidden]
    late = late[: 5 * own].reshape(5, own)
    return (
        layer_output,
        input_grad,
        qkv_weight_grad,
        late[3],
        late[4],
        attn_weight_grad,
        late[2],
        late[0],
        late[1],
        inner_rows_grad,
        inner_bias_grad,
        outer_weight_grad,
        outer_bias_grad,
        second_gain_grad,
        second_shift_grad,
    )


def solution(mesh):
    in_specs = (
        P(("replica", "group"), None),
        P("group", None),
        P("group"),
        P("group"),
        P("group", None),
        P("group"),
        P("group"),
        P("group"),
        P("group", None),
        P("group"),
        P("group", None),
        P("group"),
        P("group"),
        P("group"),
        P("replica"),
        P(("replica", "group"), None),
    )
    out_specs = (
        P(("replica", "group"), None),
        P(("replica", "group"), None),
        P("group", None),
        P("group"),
        P("group"),
        P("group", None),
        P("group"),
        P("group"),
        P("group"),
        P("group", None),
        P("group"),
        P("group", None),
        P("group"),
        P("group"),
        P("group"),
    )
    return jax.shard_map(
        on_device, mesh=mesh, in_specs=in_specs, out_specs=out_specs, check_vma=False
    )
```
